512 devices in a mesh: leaf: 512 (over z, y, x, core).
Axes of the slice: x: 4, y: 8, z: 8, core: 2. Of those that a mesh axis runs over, the one named last changes fastest.
Arguments:
- right_side_block: bfloat16 [262144, 128], P('leaf'), may hold values from -6 to 6
- leaf_rows: bfloat16 [262144, 4096], P('leaf'), as said below
- bases: bfloat16 [6, 262144, 128], P(None, 'leaf'), as said below
Outputs:
- product: float32 [262144, 128], P('leaf')
The draws below stay inside these ranges and needn't reach their ends.
Inputs may be any that keep to these rules, and one draw needn't show every extreme that they name: `leaf_rows`: within each leaf the diagonal block is symmetric: row a, column b of leaf n equals row b, column a of leaf n. `bases`: rows of independent entries; each level has its own scale.
All inputs are finite; a program needn't handle non-finite values.
Results may differ from the reference program's by a relative error of at most 0.0025.
Values may be sent and summed in bfloat16 or wider, within the bound.
No kernel may reach another device: no remote copies, remote signals or barrier semaphores. Data moves between devices by JAX's collectives and lax.ppermute only.
A program may use at most 64 MiB of HBM per device.

```python
import math
import jax
import jax.numpy as jnp
from jax import lax

LEAF = 4096
RANK = 128
RHS = 128
NLEAF = 64
POINTS = 262144
LEVELS = 6


def draw_leaf_rows(key, part):
    key = jax.random.fold_in(key, 11)
    normals = jax.random.normal(key, (NLEAF, LEAF, LEAF), jnp.float32)
    symmetric = (normals + jnp.swapaxes(normals, 1, 2)) * (0.70710678 / math.sqrt(LEAF))
    symmetric = symmetric + jnp.eye(LEAF, dtype=jnp.float32)[None, :, :]
    return symmetric.reshape(NLEAF * LEAF, LEAF).astype(jnp.bfloat16)


def draw_bases(key, part):
    key = jax.random.fold_in(key, 23)
    normals = jax.random.normal(key, (LEVELS, POINTS, RANK), jnp.float32)
    level_scale = (RANK * LEAF * 2.0 ** jnp.arange(LEVELS, dtype=jnp.float32)) ** (-0.25)
    return (normals * level_scale[:, None, None]).astype(jnp.bfloat16)


def steps_of(key, shape, split, low, top_value):
    gain, own = 1.0, jax.random.fold_in(key, 6)
    for dim, blocks in split:
        steps = jnp.exp(jax.random.uniform(jax.random.fold_in(own, dim), (blocks,), jnp.float32, low / len(split), top_value / len(split)))
        gain = gain * jnp.repeat(steps, shape[dim] // blocks).reshape([-1 if axis == dim else 1 for axis in range(len(shape))])
    return gain


def noise(rng, extent, scale, limit, split=(), kind=jnp.bfloat16):
    level = steps_of(rng, extent, split, -0.22, 0.18) if split else 1.0
    array = jax.random.normal(rng, extent, jnp.float32) * scale * level
    return jnp.minimum(jnp.maximum(array, -limit), limit).astype(kind)


def setup_inputs(seed: int = 0) -> dict:
    seeds = jax.random.split(jax.random.key(seed), 4)
    right_side_block = noise(seeds[0], (POINTS, RHS), 1.0, 6.0, ((0, 512),))
    leaf_rows = draw_leaf_rows(jax.random.fold_in(seeds[3], 71), 0)
    bases = draw_bases(jax.random.fold_in(seeds[3], 71), 0)
    return {"right_side_block": right_side_block, "leaf_rows": leaf_rows, "bases": bases}


def leaf_product(pair):
    return jnp.dot(pair[0], pair[1], preferred_element_type=jnp.float32)


def reference(right_side_block, leaf_rows, bases):
    point_count = right_side_block.shape[0]
    right_side_count = right_side_block.shape[1]
    leaf_count = point_count // LEAF
    blocks = leaf_rows.reshape(leaf_count, LEAF, LEAF)
    inputs = right_side_block.reshape(leaf_count, LEAF, right_side_count)
    product = lax.map(leaf_product, (blocks, inputs)).reshape(point_count, right_side_count)
    wide_inputs = right_side_block.astype(jnp.float32)
    for depth in range(LEVELS):
        node_rows = LEAF * 2 ** depth
        node_count = point_count // node_rows
        level_factor = bases[depth].astype(jnp.float32).reshape(node_count, node_rows, RANK)
        node_inputs = wide_inputs.reshape(node_count, node_rows, right_side_count)
        coefficient = jnp.einsum("nmr,nmk->nrk", level_factor, node_inputs)
        swapped = coefficient.reshape(node_count // 2, 2, RANK, right_side_count)[:, ::-1]
        swapped = swapped.reshape(node_count, RANK, right_side_count).astype(jnp.bfloat16)
        swapped = lax.optimization_barrier(swapped).astype(jnp.float32)
        coupled_product = jnp.einsum("nmr,nrk->nmk", level_factor, swapped)
        product = product + coupled_product.reshape(point_count, right_side_count)
    return product
```

```python
import jax
import jax.numpy as jnp
from jax import lax
from jax.sharding import Mesh, PartitionSpec as P

AXES = ("z", "y_hi", "y_lo", "x", "core")
LEAF = ("x", "core")
PAIR = ("y_lo", "x", "core")
FAR = ("z", "y_hi")


def shards(right_side_block, leaf_rows, bases):
    level_count, _, rank = bases.shape
    width = right_side_block.shape[1]
    pair_devices = lax.axis_size(PAIR)
    far_count = lax.axis_size(FAR)
    slice_rows = rank // pair_devices
    me = lax.axis_index(FAR)
    partial = jnp.einsum(
        "qip,iw->qpw", bases, right_side_block, preferred_element_type=jnp.float32
    )
    outgoing = partial.reshape(level_count, pair_devices, slice_rows, width).swapaxes(0, 1)
    incoming = lax.all_to_all(outgoing, PAIR, 0, 0)
    leaf_sums = incoming.reshape(2, pair_devices // 2, level_count, slice_rows, width).sum(1)
    pair_sums = leaf_sums[0] + leaf_sums[1]
    others = jnp.arange(far_count)
    level_of = jnp.zeros((far_count,), jnp.int32)
    for bit in range(level_count - 1):
        level_of = level_of + ((others ^ me) >> bit > 0).astype(jnp.int32)
    to_far = jnp.zeros((far_count, slice_rows, width), jnp.float32)
    for level in range(1, level_count):
        to_far = jnp.where((level_of == level)[:, None, None], pair_sums[level][None], to_far)
    to_far, late_rhs = lax.optimization_barrier((to_far, right_side_block))
    ring = [
        lax.ppermute(late_rhs, "x", [(i, (i - step) % 4) for i in range(4)]) for step in (1, 3, 2)
    ]
    column = jnp.stack([late_rhs, ring[0], ring[2], ring[1]])
    other = lax.ppermute(column, "core", [(0, 1), (1, 0)])
    core = lax.axis_index("core")
    both = jnp.where(
        core == 0, jnp.stack([column, other], 1), jnp.stack([other, column], 1)
    ).reshape(4, -1, width)
    place = lax.axis_index("x")
    gathered = lax.dynamic_slice_in_dim(
        jnp.concatenate([both, both]), (4 - place) % 4, 4, 0
    ).reshape(-1, width)
    diagonal_part = jnp.dot(leaf_rows, gathered, preferred_element_type=jnp.float32)
    from_far = lax.all_to_all(to_far, FAR, 0, 0)
    siblings = [
        jnp.where((level_of == level)[:, None, None], from_far, 0.0).sum(0)
        for level in range(1, level_count)
    ]
    both = jnp.stack(
        [jnp.stack([leaf_sums[1 - side, 0]] + siblings, 0) for side in range(2)], 0
    ).astype(jnp.bfloat16)
    spread = jnp.broadcast_to(
        both[:, None], (2, pair_devices // 2, level_count, slice_rows, width)
    ).reshape(pair_devices, level_count * slice_rows, width)
    spread = lax.all_to_all(spread, PAIR, 0, 0)
    weights = (
        spread.reshape(pair_devices, level_count, slice_rows, width)
        .swapaxes(0, 1)
        .reshape(level_count, rank, width)
    )
    coupled_product = jnp.einsum(
        "txv,tvu->xu", bases, weights, preferred_element_type=jnp.float32
    )
    return diagonal_part + coupled_product


def solution(mesh):
    fine = Mesh(mesh.devices.reshape(8, 4, 2, 4, 2), AXES)
    in_specs = (P(AXES, None), P(AXES, None), P(None, AXES, None))
    return jax.shard_map(
        shards, mesh=fine, in_specs=in_specs, out_specs=P(AXES, None), check_vma=False
    )
```

```python
import jax
import jax.numpy as jnp
from jax import lax
from jax.experimental import pallas as pl
from jax.experimental.pallas import tpu as pltpu
from jax.sharding import PartitionSpec as P

CHIPS = 4
LEAF_DEVS = 2 * CHIPS
PAIR_DEVS = 2 * LEAF_DEVS
LATE_PAIR = 30
LATE_PLACE = 6
VMEM = pl.BlockSpec(memory_space=pltpu.VMEM)


def call(kernel, outs, flops, *args):
    return pl.pallas_call(
        kernel,
        out_shape=outs,
        in_specs=[VMEM] * len(args),
        out_specs=jax.tree.map(lambda _: VMEM, outs),
        compiler_params=pltpu.CompilerParams(vmem_limit_bytes=16 << 20),
        cost_estimate=pl.CostEstimate(
            flops=flops,
            bytes_accessed=flops // 250 + sum(a.size * a.dtype.itemsize for a in args),
            transcendentals=0,
        ),
        name=kernel.__name__,
    )(*args)


def far_place():
    return lax.div(lax.axis_index("leaf"), PAIR_DEVS) ^ LATE_PAIR


def outer_block(place, bit):
    return ((place >> bit) ^ 1) << bit


def send_far(incoming_ref, far_ref, near_ref):
    sums = [incoming_ref[0], incoming_ref[LEAF_DEVS]]
    for k in range(1, LEAF_DEVS):
        sums[0] += incoming_ref[k]
        sums[1] += incoming_ref[LEAF_DEVS + k]
    both = sums[0] + sums[1]
    near_ref[0] = sums[1][0]
    near_ref[1] = sums[0][0]
    place = far_place()
    far_ref[place] = both[0]
    for bit in range(both.shape[0] - 1):
        span = 1 << bit
        far_ref[pl.ds(outer_block(place, bit), span)] = jnp.broadcast_to(
            both[bit + 1], (span,) + both.shape[1:]
        )


def gather_siblings(far_ref, near_ref, spread_ref):
    place = far_place()
    pieces = []
    for bit in range(far_ref.shape[0].bit_length() - 1):
        pieces.append(far_ref[pl.ds(outer_block(place, bit), 1 << bit)].sum(0))
    for side in range(2):
        block = jnp.concatenate([near_ref[side]] + pieces, 0).astype(spread_ref.dtype)
        for k in range(LEAF_DEVS):
            spread_ref[side * LEAF_DEVS + k] = block


def place_in_leaf():
    position = lax.rem(lax.axis_index("leaf"), LEAF_DEVS)
    return lax.div(position, 2), lax.rem(position, 2)


def columns(rows_ref, block, count):
    points = rows_ref.shape[0]
    start = pl.multiple_of(lax.rem(block, LEAF_DEVS) * points, points)
    return rows_ref[:, pl.ds(start, count * points)]


def early_blocks(rows_ref, own_ref, side_ref, opposite_ref, out_ref, rest_ref):
    chip, core = place_in_leaf()
    total = jnp.zeros(out_ref.shape, jnp.float32)
    for turn, block in ((0, own_ref), (1 + 2 * core, side_ref), (2, opposite_ref)):
        total += jnp.dot(
            columns(rows_ref, 2 * (chip + turn), 2),
            block[...],
            preferred_element_type=jnp.float32,
        )
    out_ref[...] = total
    rest_ref[...] = columns(rows_ref, 2 * (chip + 3 - 2 * core), 2)


def last_block(rest_ref, other_ref, early_ref, out_ref):
    out_ref[...] = early_ref[...] + jnp.dot(
        rest_ref[...], other_ref[...], preferred_element_type=jnp.float32
    )


def finish(bases_ref, spread_ref, diagonal_ref, out_ref):
    level_count = bases_ref.shape[0]
    total = diagonal_ref[...]
    slices = [spread_ref[k].astype(jnp.float32) for k in range(PAIR_DEVS)]
    deep = slices[0].shape[0] // level_count
    for level in range(0, level_count, 2):
        weights = jnp.concatenate(
            [s[l * deep : (l + 1) * deep] for l in (level, level + 1) for s in slices], 0
        ).astype(bases_ref.dtype)
        factor = jnp.concatenate([bases_ref[level], bases_ref[level + 1]], 1)
        total += jnp.dot(factor, weights, preferred_element_type=jnp.float32)
    out_ref[...] = total


def shards(right_side_block, leaf_rows, bases):
    level_count, points, rank = bases.shape
    width = right_side_block.shape[1]
    device_count = lax.axis_size("leaf")
    pair_count = device_count // PAIR_DEVS
    slice_rows = rank // PAIR_DEVS
    near = [
        [p * PAIR_DEVS + (k ^ LATE_PLACE) for k in range(PAIR_DEVS)] for p in range(pair_count)
    ]
    far = [
        [(k ^ LATE_PAIR) * PAIR_DEVS + m for k in range(pair_count)] for m in range(PAIR_DEVS)
    ]
    f32 = lambda *shape: jax.ShapeDtypeStruct(shape, jnp.float32)

    partial = jnp.einsum(
        "qip,iw->qpw", bases, right_side_block, preferred_element_type=jnp.float32
    )
    outgoing = partial.reshape(level_count, PAIR_DEVS, slice_rows, width).swapaxes(0, 1)
    incoming = lax.all_to_all(outgoing, "leaf", 0, 0, axis_index_groups=near)

    swap = [(i, i ^ 1) for i in range(device_count)]
    twin = lax.ppermute(right_side_block, "leaf", swap)
    own = jnp.where(
        lax.axis_index("leaf") % 2 == 0,
        jnp.concatenate([right_side_block, twin]),
        jnp.concatenate([twin, right_side_block]),
    )
    to_far, beside = call(
        send_far, (f32(pair_count, slice_rows, width), f32(2, slice_rows, width)), 0, incoming
    )
    to_far, own = lax.optimization_barrier((to_far, own))
    from_far = lax.all_to_all(to_far, "leaf", 0, 0, axis_index_groups=far)
    leaf_of = lambda i: i // LEAF_DEVS * LEAF_DEVS
    beyond = [
        lax.ppermute(
            own, "leaf", [(i, leaf_of(i) + (i + step[i % 2]) % LEAF_DEVS) for i in range(device_count)]
        )
        for step in ((-2, 2), (4, 4))
    ]
    spread = call(
        gather_siblings,
        jax.ShapeDtypeStruct((PAIR_DEVS, level_count * slice_rows, width), bases.dtype),
        0,
        from_far,
        beside,
    )
    spread = lax.all_to_all(spread, "leaf", 0, 0, axis_index_groups=near)

    side, opposite = lax.optimization_barrier(tuple(beyond))
    other = lax.ppermute(side, "leaf", swap)
    early, rest = call(
        early_blocks,
        (f32(points, width), jax.ShapeDtypeStruct((points, 2 * points), bases.dtype)),
        0 * leaf_rows.size * width,
        leaf_rows,
        own,
        side,
        opposite,
    )
    product = call(last_block, f32(points, width), 0, rest, other, early)
    return call(finish, f32(points, width), bases.size * width, bases, spread, product)


def solution(mesh):
    in_specs = (P("leaf", None), P("leaf", None), P(None, "leaf", None))
    return jax.shard_map(
        shards, mesh=mesh, in_specs=in_specs, out_specs=P("leaf", None), check_vma=False
    )
```

```python
import jax
import jax.numpy as jnp
from jax import lax
from jax.experimental import pallas as pl
from jax.experimental.pallas import tpu as pltpu
from jax.sharding import PartitionSpec as P

CHIPS = 4
LEAF_DEVS = 2 * CHIPS
PAIR_DEVS = 2 * LEAF_DEVS
LATE_PAIR = 30
LATE_PLACE = 6
VMEM = pl.BlockSpec(memory_space=pltpu.VMEM)


def call(kernel, outs, flops, *args):
    return pl.pallas_call(
        kernel,
        out_shape=outs,
        in_specs=[VMEM] * len(args),
        out_specs=jax.tree.map(lambda _: VMEM, outs),
        compiler_params=pltpu.CompilerParams(vmem_limit_bytes=16 << 20),
        cost_estimate=pl.CostEstimate(
            flops=flops,
            bytes_accessed=flops // 250 + sum(a.size * a.dtype.itemsize for a in args),
            transcendentals=0,
        ),
        name=kernel.__name__,
    )(*args)


def far_place():
    return lax.div(lax.axis_index("leaf"), PAIR_DEVS) ^ LATE_PAIR


def outer_block(place, bit):
    return ((place >> bit) ^ 1) << bit


def send_far(incoming_ref, far_ref, near_ref):
    sums = [incoming_ref[0], incoming_ref[LEAF_DEVS]]
    for k in range(1, LEAF_DEVS):
        sums[0] += incoming_ref[k]
        sums[1] += incoming_ref[LEAF_DEVS + k]
    both = sums[0] + sums[1]
    near_ref[0] = sums[1][0]
    near_ref[1] = sums[0][0]
    place = far_place()
    far_ref[place] = both[0]
    for bit in range(both.shape[0] - 1):
        span = 1 << bit
        far_ref[pl.ds(outer_block(place, bit), span)] = jnp.broadcast_to(
            both[bit + 1], (span,) + both.shape[1:]
        )


def gather_siblings(far_ref, near_ref, spread_ref):
    place = far_place()
    pieces = []
    for bit in range(far_ref.shape[0].bit_length() - 1):
        pieces.append(far_ref[pl.ds(outer_block(place, bit), 1 << bit)].sum(0))
    for side in range(2):
        block = jnp.concatenate([near_ref[side]] + pieces, 0).astype(spread_ref.dtype)
        for k in range(LEAF_DEVS):
            spread_ref[side * LEAF_DEVS + k] = block


def place_in_leaf():
    position = lax.rem(lax.axis_index("leaf"), LEAF_DEVS)
    return lax.div(position, 2), lax.rem(position, 2)


def columns(rows_ref, block, count):
    points = rows_ref.shape[0]
    start = pl.multiple_of(lax.rem(block, LEAF_DEVS) * points, points)
    return rows_ref[:, pl.ds(start, count * points)]


def early_blocks(rows_ref, own_ref, side_ref, opposite_ref, out_ref, rest_ref):
    chip, core = place_in_leaf()
    total = jnp.zeros(out_ref.shape, jnp.float32)
    for turn, block in ((0, own_ref), (1 + 2 * core, side_ref), (2, opposite_ref)):
        total += jnp.dot(
            columns(rows_ref, 2 * (chip + turn), 2),
            block[...],
            preferred_element_type=jnp.float32,
        )
    out_ref[...] = total
    rest_ref[...] = columns(rows_ref, 2 * (chip + 3 - 2 * core), 2)


def last_block(rest_ref, other_ref, early_ref, out_ref):
    out_ref[...] = early_ref[...] + jnp.dot(
        rest_ref[...], other_ref[...], preferred_element_type=jnp.float32
    )


def finish(bases_ref, spread_ref, diagonal_ref, out_ref):
    level_count = bases_ref.shape[0]
    total = diagonal_ref[...]
    slices = [spread_ref[k].astype(jnp.float32) for k in range(PAIR_DEVS)]
    deep = slices[0].shape[0] // level_count
    for level in range(0, level_count, 2):
        weights = jnp.concatenate(
            [s[l * deep : (l + 1) * deep] for l in (level, level + 1) for s in slices], 0
        ).astype(bases_ref.dtype)
        factor = jnp.concatenate([bases_ref[level], bases_ref[level + 1]], 1)
        total += jnp.dot(factor, weights, preferred_element_type=jnp.float32)
    out_ref[...] = total


def shards(right_side_block, leaf_rows, bases):
    level_count, points, rank = bases.shape
    width = right_side_block.shape[1]
    device_count = lax.axis_size("leaf")
    pair_count = device_count // PAIR_DEVS
    slice_rows = rank // PAIR_DEVS
    near = [
        [p * PAIR_DEVS + (k ^ LATE_PLACE) for k in range(PAIR_DEVS)] for p in range(pair_count)
    ]
    far = [
        [(k ^ LATE_PAIR) * PAIR_DEVS + m for k in range(pair_count)] for m in range(PAIR_DEVS)
    ]
    f32 = lambda *shape: jax.ShapeDtypeStruct(shape, jnp.float32)

    partial = jnp.einsum(
        "qip,iw->qpw", bases, right_side_block, preferred_element_type=jnp.float32
    )
    largest = jnp.max(jnp.abs(partial), axis=(1, 2))
    power = 14.0 - jnp.ceil(jnp.log2(jnp.maximum(largest, 1e-30)))
    scaled = (partial * jnp.exp2(power)[:, None, None]).astype(jnp.float16)
    powers = jnp.broadcast_to(
        jnp.pad(power, (0, slice_rows - level_count))[None, :, None],
        (PAIR_DEVS, slice_rows, width),
    ).astype(jnp.float16)
    outgoing = scaled.reshape(level_count, PAIR_DEVS, slice_rows, width).swapaxes(0, 1)
    outgoing = jnp.concatenate(
        [outgoing.reshape(PAIR_DEVS, level_count * slice_rows, width), powers], 1
    )
    received = lax.all_to_all(outgoing, "leaf", 0, 0, axis_index_groups=near)
    received = received.astype(jnp.float32)
    undo = jnp.exp2(-received[:, level_count * slice_rows :][:, :level_count])
    incoming = (
        received[:, : level_count * slice_rows].reshape(
            PAIR_DEVS, level_count, slice_rows, width
        )
        * undo[:, :, None, :]
    )
    swap = [(i, i ^ 1) for i in range(device_count)]
    twin = lax.ppermute(right_side_block, "leaf", swap)
    own = jnp.where(
        lax.axis_index("leaf") % 2 == 0,
        jnp.concatenate([right_side_block, twin]),
        jnp.concatenate([twin, right_side_block]),
    )
    to_far, beside = call(
        send_far, (f32(pair_count, slice_rows, width), f32(2, slice_rows, width)), 0, incoming
    )
    to_far, own = lax.optimization_barrier((to_far, own))
    from_far = lax.all_to_all(to_far, "leaf", 0, 0, axis_index_groups=far)
    leaf_of = lambda i: i // LEAF_DEVS * LEAF_DEVS
    beyond = [
        lax.ppermute(
            own, "leaf", [(i, leaf_of(i) + (i + step[i % 2]) % LEAF_DEVS) for i in range(device_count)]
        )
        for step in ((4, 4), (-2, 2))
    ]
    spread = call(
        gather_siblings,
        jax.ShapeDtypeStruct((PAIR_DEVS, level_count * slice_rows, width), bases.dtype),
        0,
        from_far,
        beside,
    )
    spread = lax.all_to_all(spread, "leaf", 0, 0, axis_index_groups=near)

    opposite, side = lax.optimization_barrier(tuple(beyond))
    other = lax.ppermute(side, "leaf", swap)
    early, rest = call(
        early_blocks,
        (f32(points, width), jax.ShapeDtypeStruct((points, 2 * points), bases.dtype)),
        0 * leaf_rows.size * width,
        leaf_rows,
        own,
        side,
        opposite,
    )
    product = call(last_block, f32(points, width), 0, rest, other, early)
    return call(finish, f32(points, width), bases.size * width, bases, spread, product)


def solution(mesh):
    in_specs = (P("leaf", None), P("leaf", None), P(None, "leaf", None))
    return jax.shard_map(
        shards, mesh=mesh, in_specs=in_specs, out_specs=P("leaf", None), check_vma=False
    )
```

```python
import jax
import jax.numpy as jnp
from jax import lax
from jax.experimental import pallas as pl
from jax.experimental.pallas import tpu as pltpu
from jax.sharding import PartitionSpec as P

CHIPS = 4
LEAF_DEVS = 2 * CHIPS
PAIR_DEVS = 2 * LEAF_DEVS
LATE_PAIR = 30
LATE_PLACE = 6
VMEM = pl.BlockSpec(memory_space=pltpu.VMEM)


def call(kernel, outs, flops, *args):
    return pl.pallas_call(
        kernel,
        out_shape=outs,
        in_specs=[VMEM] * len(args),
        out_specs=jax.tree.map(lambda _: VMEM, outs),
        compiler_params=pltpu.CompilerParams(vmem_limit_bytes=16 << 20),
        cost_estimate=pl.CostEstimate(
            flops=flops,
            bytes_accessed=flops // 250 + sum(a.size * a.dtype.itemsize for a in args),
            transcendentals=0,
        ),
        name=kernel.__name__,
    )(*args)


def far_place():
    return lax.div(lax.axis_index("leaf"), PAIR_DEVS) ^ LATE_PAIR


def outer_block(place, bit):
    return ((place >> bit) ^ 1) << bit


def send_far(incoming_ref, far_ref, near_ref):
    sums = [incoming_ref[0], incoming_ref[LEAF_DEVS]]
    for k in range(1, LEAF_DEVS):
        sums[0] += incoming_ref[k]
        sums[1] += incoming_ref[LEAF_DEVS + k]
    both = sums[0] + sums[1]
    near_ref[0] = sums[1][0]
    near_ref[1] = sums[0][0]
    place = far_place()
    far_ref[place] = both[0]
    for bit in range(both.shape[0] - 1):
        span = 1 << bit
        far_ref[pl.ds(outer_block(place, bit), span)] = jnp.broadcast_to(
            both[bit + 1], (span,) + both.shape[1:]
        )


def gather_siblings(far_ref, near_ref, spread_ref):
    place = far_place()
    pieces = []
    for bit in range(far_ref.shape[0].bit_length() - 1):
        pieces.append(far_ref[pl.ds(outer_block(place, bit), 1 << bit)].sum(0))
    for side in range(2):
        block = jnp.concatenate([near_ref[side]] + pieces, 0).astype(spread_ref.dtype)
        for k in range(LEAF_DEVS):
            spread_ref[side * LEAF_DEVS + k] = block


def place_in_leaf():
    position = lax.rem(lax.axis_index("leaf"), LEAF_DEVS)
    return lax.div(position, 2), lax.rem(position, 2)


def columns(rows_ref, block, count):
    points = rows_ref.shape[0]
    start = pl.multiple_of(lax.rem(block, LEAF_DEVS) * points, points)
    return rows_ref[:, pl.ds(start, count * points)]


def early_blocks(rows_ref, own_ref, side_ref, opposite_ref, out_ref, rest_ref):
    chip, core = place_in_leaf()
    total = jnp.zeros(out_ref.shape, jnp.float32)
    for turn, block in ((0, own_ref), (1 + 2 * core, side_ref), (2, opposite_ref)):
        total += jnp.dot(
            columns(rows_ref, 2 * (chip + turn), 2),
            block[...],
            preferred_element_type=jnp.float32,
        )
    out_ref[...] = total
    rest_ref[...] = columns(rows_ref, 2 * (chip + 3 - 2 * core), 2)


def finish(rest_ref, other_ref, early_ref, bases_ref, spread_ref, out_ref):
    level_count = bases_ref.shape[0]
    total = early_ref[...] + jnp.dot(
        rest_ref[...], other_ref[...], preferred_element_type=jnp.float32
    )
    slices = [spread_ref[k].astype(jnp.float32) for k in range(PAIR_DEVS)]
    deep = slices[0].shape[0] // level_count
    for level in range(0, level_count, 2):
        weights = jnp.concatenate(
            [s[l * deep : (l + 1) * deep] for l in (level, level + 1) for s in slices], 0
        ).astype(bases_ref.dtype)
        factor = jnp.concatenate([bases_ref[level], bases_ref[level + 1]], 1)
        total += jnp.dot(factor, weights, preferred_element_type=jnp.float32)
    out_ref[...] = total


def shards(right_side_block, leaf_rows, bases):
    level_count, points, rank = bases.shape
    width = right_side_block.shape[1]
    device_count = lax.axis_size("leaf")
    pair_count = device_count // PAIR_DEVS
    slice_rows = rank // PAIR_DEVS
    near = [
        [p * PAIR_DEVS + (k ^ LATE_PLACE) for k in range(PAIR_DEVS)] for p in range(pair_count)
    ]
    far = [
        [(k ^ LATE_PAIR) * PAIR_DEVS + m for k in range(pair_count)] for m in range(PAIR_DEVS)
    ]
    f32 = lambda *shape: jax.ShapeDtypeStruct(shape, jnp.float32)

    partial = jnp.einsum(
        "qip,iw->qpw", bases, right_side_block, preferred_element_type=jnp.float32
    )
    largest = jnp.max(jnp.abs(partial), axis=(1, 2))
    power = 14.0 - jnp.ceil(jnp.log2(jnp.maximum(largest, 1e-30)))
    powers = jnp.tile(jnp.pad(power, (0, slice_rows - level_count)), PAIR_DEVS)
    outgoing = jnp.concatenate(
        [
            partial * jnp.exp2(power)[:, None, None],
            jnp.broadcast_to(powers[None, :, None], (1, rank, width)),
        ],
        0,
    )
    outgoing = (
        outgoing.reshape(level_count + 1, PAIR_DEVS, slice_rows, width)
        .swapaxes(0, 1)
        .reshape(PAIR_DEVS, (level_count + 1) * slice_rows, width)
        .astype(jnp.float16)
    )
    received = lax.all_to_all(outgoing, "leaf", 0, 0, axis_index_groups=near)
    received = received.astype(jnp.float32)
    undo = jnp.exp2(-received[:, level_count * slice_rows :][:, :level_count])
    incoming = (
        received[:, : level_count * slice_rows].reshape(
            PAIR_DEVS, level_count, slice_rows, width
        )
        * undo[:, :, None, :]
    )
    swap = [(i, i ^ 1) for i in range(device_count)]
    twin = lax.ppermute(right_side_block, "leaf", swap)
    own = jnp.where(
        lax.axis_index("leaf") % 2 == 0,
        jnp.concatenate([right_side_block, twin]),
        jnp.concatenate([twin, right_side_block]),
    )
    to_far, beside = call(
        send_far, (f32(pair_count, slice_rows, width), f32(2, slice_rows, width)), 0, incoming
    )
    to_far, own = lax.optimization_barrier((to_far, own))
    from_far = lax.all_to_all(to_far, "leaf", 0, 0, axis_index_groups=far)
    leaf_of = lambda i: i // LEAF_DEVS * LEAF_DEVS
    beyond = [
        lax.ppermute(
            own, "leaf", [(i, leaf_of(i) + (i + step[i % 2]) % LEAF_DEVS) for i in range(device_count)]
        )
        for step in ((4, 4), (-2, 2))
    ]
    spread = call(
        gather_siblings,
        jax.ShapeDtypeStruct((PAIR_DEVS, level_count * slice_rows, width), bases.dtype),
        0,
        from_far,
        beside,
    )
    spread = lax.all_to_all(spread, "leaf", 0, 0, axis_index_groups=near)

    opposite, side = lax.optimization_barrier(tuple(beyond))
    other = lax.ppermute(side, "leaf", swap)
    early, rest = call(
        early_blocks,
        (f32(points, width), jax.ShapeDtypeStruct((points, 2 * points), bases.dtype)),
        0 * leaf_rows.size * width,
        leaf_rows,
        own,
        side,
        opposite,
    )
    return call(finish, f32(points, width), 0, rest, other, early, bases, spread)


def solution(mesh):
    in_specs = (P("leaf", None), P("leaf", None), P(None, "leaf", None))
    return jax.shard_map(
        shards, mesh=mesh, in_specs=in_specs, out_specs=P("leaf", None), check_vma=False
    )
```

```python
import jax
import jax.numpy as jnp
from jax import lax
from jax.experimental import pallas as pl
from jax.experimental.pallas import tpu as pltpu
from jax.sharding import PartitionSpec as P

CHIPS = 4
LEAF_DEVS = 2 * CHIPS
PAIR_DEVS = 2 * LEAF_DEVS
LATE_PAIR = 22
LATE_PLACE = 6
VMEM = pl.BlockSpec(memory_space=pltpu.VMEM)


def call(kernel, outs, flops, *args):
    return pl.pallas_call(
        kernel,
        out_shape=outs,
        in_specs=[VMEM] * len(args),
        out_specs=jax.tree.map(lambda _: VMEM, outs),
        compiler_params=pltpu.CompilerParams(vmem_limit_bytes=16 << 20),
        cost_estimate=pl.CostEstimate(
            flops=flops,
            bytes_accessed=flops // 250 + sum(a.size * a.dtype.itemsize for a in args),
            transcendentals=0,
        ),
        name=kernel.__name__,
    )(*args)


def far_place():
    return lax.div(lax.axis_index("leaf"), PAIR_DEVS) ^ LATE_PAIR


def outer_block(place, bit):
    return ((place >> bit) ^ 1) << bit


def send_far(incoming_ref, far_ref, near_ref):
    sums = [incoming_ref[0], incoming_ref[LEAF_DEVS]]
    for k in range(1, LEAF_DEVS):
        sums[0] += incoming_ref[k]
        sums[1] += incoming_ref[LEAF_DEVS + k]
    both = sums[0] + sums[1]
    near_ref[0] = sums[1][0]
    near_ref[1] = sums[0][0]
    place = far_place()
    far_ref[place] = both[0]
    for bit in range(both.shape[0] - 1):
        span = 1 << bit
        far_ref[pl.ds(outer_block(place, bit), span)] = jnp.broadcast_to(
            both[bit + 1], (span,) + both.shape[1:]
        )


def gather_siblings(far_ref, near_ref, spread_ref):
    place = far_place()
    pieces = []
    for bit in range(far_ref.shape[0].bit_length() - 1):
        pieces.append(far_ref[pl.ds(outer_block(place, bit), 1 << bit)].sum(0))
    for side in range(2):
        block = jnp.concatenate([near_ref[side]] + pieces, 0).astype(spread_ref.dtype)
        for k in range(LEAF_DEVS):
            spread_ref[side * LEAF_DEVS + k] = block


def place_in_leaf():
    position = lax.rem(lax.axis_index("leaf"), LEAF_DEVS)
    return lax.div(position, 2), lax.rem(position, 2)


def columns(rows_ref, block, count):
    points = rows_ref.shape[0]
    start = pl.multiple_of(lax.rem(block, LEAF_DEVS) * points, points)
    return rows_ref[:, pl.ds(start, count * points)]


def early_blocks(rows_ref, own_ref, side_ref, opposite_ref, out_ref, rest_ref):
    chip, core = place_in_leaf()
    total = jnp.zeros(out_ref.shape, jnp.float32)
    for turn, block in ((0, own_ref), (1 + 2 * core, side_ref), (2, opposite_ref)):
        total += jnp.dot(
            columns(rows_ref, 2 * (chip + turn), 2),
            block[...],
            preferred_element_type=jnp.float32,
        )
    out_ref[...] = total
    rest_ref[...] = columns(rows_ref, 2 * (chip + 3 - 2 * core), 2)


def finish(rest_ref, other_ref, early_ref, bases_ref, spread_ref, out_ref):
    level_count = bases_ref.shape[0]
    total = early_ref[...] + jnp.dot(
        rest_ref[...], other_ref[...], preferred_element_type=jnp.float32
    )
    slices = [spread_ref[k].astype(jnp.float32) for k in range(PAIR_DEVS)]
    deep = slices[0].shape[0] // level_count
    for level in range(0, level_count, 2):
        weights = jnp.concatenate(
            [s[l * deep : (l + 1) * deep] for l in (level, level + 1) for s in slices], 0
        ).astype(bases_ref.dtype)
        factor = jnp.concatenate([bases_ref[level], bases_ref[level + 1]], 1)
        total += jnp.dot(factor, weights, preferred_element_type=jnp.float32)
    out_ref[...] = total


def shards(right_side_block, leaf_rows, bases):
    level_count, points, rank = bases.shape
    width = right_side_block.shape[1]
    device_count = lax.axis_size("leaf")
    pair_count = device_count // PAIR_DEVS
    slice_rows = rank // PAIR_DEVS
    near = [
        [p * PAIR_DEVS + (k ^ LATE_PLACE) for k in range(PAIR_DEVS)] for p in range(pair_count)
    ]
    far = [
        [(k ^ LATE_PAIR) * PAIR_DEVS + m for k in range(pair_count)] for m in range(PAIR_DEVS)
    ]
    f32 = lambda *shape: jax.ShapeDtypeStruct(shape, jnp.float32)

    partial = jnp.einsum(
        "qip,iw->qpw", bases, right_side_block, preferred_element_type=jnp.float32
    )
    largest = jnp.max(jnp.abs(partial), axis=(1, 2))
    power = 14.0 - jnp.ceil(jnp.log2(jnp.maximum(largest, 1e-30)))
    powers = jnp.tile(jnp.pad(power, (0, slice_rows - level_count)), PAIR_DEVS)
    outgoing = jnp.concatenate(
        [
            partial * jnp.exp2(power)[:, None, None],
            jnp.broadcast_to(powers[None, :, None], (1, rank, width)),
        ],
        0,
    )
    outgoing = (
        outgoing.reshape(level_count + 1, PAIR_DEVS, slice_rows, width)
        .swapaxes(0, 1)
        .reshape(PAIR_DEVS, (level_count + 1) * slice_rows, width)
        .astype(jnp.float16)
    )
    received = lax.all_to_all(outgoing, "leaf", 0, 0, axis_index_groups=near)
    received = received.astype(jnp.float32)
    undo = jnp.exp2(-received[:, level_count * slice_rows :][:, :level_count])
    incoming = (
        received[:, : level_count * slice_rows].reshape(
            PAIR_DEVS, level_count, slice_rows, width
        )
        * undo[:, :, None, :]
    )
    swap = [(i, i ^ 1) for i in range(device_count)]
    twin = lax.ppermute(right_side_block, "leaf", swap)
    own = jnp.where(
        lax.axis_index("leaf") % 2 == 0,
        jnp.concatenate([right_side_block, twin]),
        jnp.concatenate([twin, right_side_block]),
    )
    to_far, beside = call(
        send_far, (f32(pair_count, slice_rows, width), f32(2, slice_rows, width)), 0, incoming
    )
    to_far, own = lax.optimization_barrier((to_far, own))
    from_far = lax.all_to_all(to_far, "leaf", 0, 0, axis_index_groups=far)
    leaf_of = lambda i: i // LEAF_DEVS * LEAF_DEVS
    beyond = [
        lax.ppermute(
            own, "leaf", [(i, leaf_of(i) + (i + step[i % 2]) % LEAF_DEVS) for i in range(device_count)]
        )
        for step in ((4, 4), (-2, 2))
    ]
    spread = call(
        gather_siblings,
        jax.ShapeDtypeStruct((PAIR_DEVS, level_count * slice_rows, width), bases.dtype),
        0,
        from_far,
        beside,
    )
    spread = lax.all_to_all(spread, "leaf", 0, 0, axis_index_groups=near)

    opposite, side = lax.optimization_barrier(tuple(beyond))
    other = lax.ppermute(side, "leaf", swap)
    early, rest = call(
        early_blocks,
        (f32(points, width), jax.ShapeDtypeStruct((points, 2 * points), bases.dtype)),
        0 * leaf_rows.size * width,
        leaf_rows,
        own,
        side,
        opposite,
    )
    return call(finish, f32(points, width), 0, rest, other, early, bases, spread)


def solution(mesh):
    in_specs = (P("leaf", None), P("leaf", None), P(None, "leaf", None))
    return jax.shard_map(
        shards, mesh=mesh, in_specs=in_specs, out_specs=P("leaf", None), check_vma=False
    )
```
